256 devices in a mesh: ctx: 32 (over z_lo, x, core), ch: 8 (over z_hi, y).
Axes of the slice: x: 4, y: 4, z: 8 (z_hi: 2, z_lo: 4; z = z_hi * 4 + z_lo), core: 2. Of those that a mesh axis runs over, the one named last changes fastest.
Arguments:
- stream: bfloat16 [8192, 8192], P('ctx', 'ch'), may hold values from -6 to 6
- projected: bfloat16 [8192, 3, 8192], P('ctx', None, 'ch'), may hold values from -6 to 6
- short_taps: float32 [3, 3, 8192], P(None, None, 'ch'), may hold values from -3 to 3
- decay_rates: float32 [16, 8192], P(None, 'ch'), may hold values from 3.0517578e-05 to 0.05, as said below
- residues: float32 [16, 8192], P(None, 'ch'), may hold values from -0.5 to 0.5
- out_weight: bfloat16 [8192, 8192], P('ctx', 'ch'), may hold values from -0.0625 to 0.0625
Outputs:
- block_out: bfloat16 [8192, 8192], P('ctx', 'ch')
The draws below stay inside these ranges and needn't reach their ends.
Inputs may be any that keep to these rules, and one draw needn't show every extreme that they name: `decay_rates`: rates of each channel's modes.
All inputs are finite; a program needn't handle non-finite values.
Results may differ from the reference program's by a relative error of at most 0.009.
Values may be sent and summed in bfloat16 or wider, within the bound.
No kernel may reach another device: no remote copies, remote signals or barrier semaphores. Data moves between devices by JAX's collectives and lax.ppermute only.
A program may use at most 128 MiB of HBM per device.

```python
import jax
import jax.numpy as jnp
from jax import lax

D = 8192
MODES = 16
TOKENS = 8192


def mode_rates(key, upper):
    lower = 0.25 / TOKENS
    unit = jax.random.uniform(key, (MODES, D), jnp.float32)
    return lower * jnp.exp(unit * jnp.log(upper / lower))


def draw_decay_rates(key, part):
    upper = 0.05
    rates = mode_rates(key, upper)
    return rates


def draw_residues(key, part):
    upper = 0.05
    rates = mode_rates(key, upper)
    key = jax.random.fold_in(key, 5)
    base = jnp.clip(jax.random.normal(key, (MODES, D), jnp.float32), -4.0, 4.0)
    return base * jnp.sqrt(2.0 * rates / MODES)


def block_levels(rng, shape, cuts, least, largest):
    gain = 1.0
    for position, blocks in cuts:
        draws = jax.random.uniform(jax.random.fold_in(jax.random.fold_in(rng, 6), position), (blocks,), jnp.float32, least / len(cuts), largest / len(cuts))
        gain = gain * jnp.repeat(jnp.exp(draws), shape[position] // blocks).reshape((-1,) + (1,) * (len(shape) - 1 - position))
    return gain


def noise(rng, shape, deviation, most, shards=(), kind=jnp.bfloat16):
    array = jax.random.normal(rng, shape, jnp.float32) * deviation
    if len(shards) > 0:
        array = block_levels(rng, shape, shards, -0.22, 0.18) * array
    return jnp.clip(array, min=-most, max=most).astype(kind)


def setup_inputs(seed: int = 0) -> dict:
    key_of = jax.random.split(jax.random.key(seed), 7)
    stream = noise(key_of[0], (TOKENS, D), 1.0, 6.0, ((0, 32), (1, 8)))
    projected = noise(key_of[1], (TOKENS, 3, D), 1.0, 6.0, ((0, 32), (2, 8)))
    short_taps = noise(key_of[2], (3, 3, D), 0.6, 3.0, ((2, 8),), jnp.float32)
    decay_rates = draw_decay_rates(jax.random.fold_in(key_of[6], 71), 0)
    residues = draw_residues(jax.random.fold_in(key_of[6], 71), 0)
    out_weight = noise(key_of[5], (D, D), D ** -0.5, 0.0625, ((0, 32), (1, 8)))
    return {"stream": stream, "projected": projected, "short_taps": short_taps, "decay_rates": decay_rates, "residues": residues, "out_weight": out_weight}


def reference(stream, projected, short_taps, decay_rates, residues, out_weight):
    seq_length = stream.shape[0]
    chan_width = stream.shape[1]
    streams = projected.astype(jnp.float32)
    zero_row = jnp.zeros((1,) + streams.shape[1:], jnp.float32)
    back_one = jnp.concatenate([zero_row, streams[:-1]], axis=0)
    back_two = jnp.concatenate([zero_row, back_one[:-1]], axis=0)
    filtered = short_taps[0] * streams + short_taps[1] * back_one + short_taps[2] * back_two
    queries = filtered[:, 0]
    drive_field = filtered[:, 1] * filtered[:, 2]
    block_width = 512 if chan_width % 512 == 0 else chan_width
    block_count = chan_width // block_width
    positions = jnp.arange(seq_length, dtype=jnp.float32)

    def convolve(operands):
        drive_block, rates_block, weights_block = operands
        kernel = jnp.zeros((seq_length, block_width), jnp.float32)
        for mode_index in range(MODES):
            kernel = kernel + weights_block[mode_index] * jnp.exp(-rates_block[mode_index] * positions[:, None])
        product = jnp.fft.rfft(kernel, n=2 * seq_length, axis=0) * jnp.fft.rfft(drive_block, n=2 * seq_length, axis=0)
        return jnp.fft.irfft(product, n=2 * seq_length, axis=0)[:seq_length].astype(jnp.float32)

    drive_blocks = drive_field.reshape(seq_length, block_count, block_width).transpose(1, 0, 2)
    rate_blocks = decay_rates.reshape(MODES, block_count, block_width).transpose(1, 0, 2)
    weight_blocks = residues.reshape(MODES, block_count, block_width).transpose(1, 0, 2)
    response = lax.map(convolve, (drive_blocks, rate_blocks, weight_blocks))
    response = response.transpose(1, 0, 2).reshape(seq_length, chan_width)
    gated_rows = (queries * response).astype(jnp.bfloat16)
    summed = stream.astype(jnp.float32) + jnp.dot(gated_rows, out_weight, preferred_element_type=jnp.float32)
    return summed.astype(jnp.bfloat16)
```

```python
import functools

import jax
import jax.numpy as jnp
from jax import lax
from jax.experimental import pallas as pl
from jax.experimental.pallas import tpu as pltpu
from jax.sharding import PartitionSpec as P

F32, BF16 = jnp.float32, jnp.bfloat16
ZL, X, CORE, ZH, Y = 4, 4, 2, 2, 4
ROWS, CHANS, MODES = 256, 1024, 16
LANES = CHANS // 128
PITCH = ROWS + 8
HALF = CHANS // 2
VMEM_LIMIT = 48 * 1024 * 1024


def ctx_pairs(move):
    pairs = []
    for p in range(ZL * X * CORE):
        target = move(p // (X * CORE), (p // CORE) % X, p % CORE)
        if target is not None:
            z, x, c = target
            pairs.append((p, (z * X + x) * CORE + c))
    return pairs


def ch_pairs(move):
    pairs = []
    for q in range(ZH * Y):
        h, y = move(q // Y, q % Y)
        pairs.append((q, h * Y + y))
    return pairs


def swap_core(v):
    return lax.ppermute(v, "ctx", ctx_pairs(lambda z, x, c: (z, x, 1 - c)))


def shift_x(v, by):
    return lax.ppermute(v, "ctx", ctx_pairs(lambda z, x, c: (z, (x + by) % X, c)))


def shift_z(v, by):
    return lax.ppermute(v, "ctx", ctx_pairs(lambda z, x, c: ((z + by) % ZL, x, c)))


def ahead_z(v, by):
    return lax.ppermute(v, "ctx", ctx_pairs(lambda z, x, c: (z + by, x, c) if z + by < ZL else None))


def swap_zh(v):
    return lax.ppermute(v, "ch", ch_pairs(lambda h, y: (1 - h, y)))


def shift_y(v, by):
    return lax.ppermute(v, "ch", ch_pairs(lambda h, y: (h, (y + by) % Y)))


def drive_kernel(proj, halo, taps, rates, drive, queries, ends, wide):
    def lane_block(j, carry):
        lanes = pl.ds(pl.multiple_of(j * 128, 128), 128)
        base = pl.multiple_of(j * PITCH, 8)
        for s in range(3):
            wide[s, 6:8, :] = halo[s, :, lanes]
            wide[s, 8:, :] = proj[s, :, lanes].astype(F32)
        step = 64
        for start in range(0, ROWS, step):
            filtered = []
            for s in range(3):
                total = taps[s : s + 1, lanes] * wide[s, 8 + start : 8 + start + step, :]
                total += taps[3 + s : 4 + s, lanes] * wide[s, 7 + start : 7 + start + step, :]
                total += taps[6 + s : 7 + s, lanes] * wide[s, 6 + start : 6 + start + step, :]
                filtered.append(total)
            queries[start : start + step, lanes] = filtered[0]
            drive[pl.ds(base + start, step), :] = filtered[1] * filtered[2]
        lam = [jnp.broadcast_to(rates[n : n + 1, lanes], (8, 128)) for n in range(MODES)]
        decay = [jnp.exp(-8.0 * lam[n]) for n in range(MODES)]

        def rows_block(b, states):
            u = drive[pl.ds(base + b * 8, 8), :]
            return tuple(states[n] * decay[n] + u for n in range(MODES))

        zero = jnp.zeros((8, 128), F32)
        states = lax.fori_loop(0, ROWS // 8, rows_block, (zero,) * MODES, unroll=4)
        left = 7.0 - lax.broadcasted_iota(jnp.int32, (8, 128), 0).astype(F32)
        for n in range(MODES):
            end = jnp.sum(states[n] * jnp.exp(-lam[n] * left), axis=0, keepdims=True)
            ends[n, pl.ds(j, 1), :] = end
        return carry

    lax.fori_loop(0, LANES, lane_block, 0)


def drive_call(proj, halo, taps, rates):
    return pl.pallas_call(
        drive_kernel,
        out_shape=(
            jax.ShapeDtypeStruct((LANES * PITCH, 128), F32),
            jax.ShapeDtypeStruct((ROWS, CHANS), F32),
            jax.ShapeDtypeStruct((MODES, LANES, 128), F32),
        ),
        scratch_shapes=[pltpu.VMEM((3, ROWS + 8, 128), F32)],
        compiler_params=pltpu.CompilerParams(vmem_limit_bytes=VMEM_LIMIT),
        cost_estimate=pl.CostEstimate(flops=30_000_000, bytes_accessed=4_000_000, transcendentals=0),
        name="drive_and_ends",
    )(proj, halo, taps, rates)


def response_kernel(place, drive, queries, rates, weights, carried, keep, send, response):
    decay = [jnp.exp(-rates[n]) for n in range(MODES)]
    gain = [weights[n] for n in range(MODES)]

    def step(t, states):
        u = drive[pl.ds(t, LANES, stride=PITCH), :]
        states = tuple(states[n] * decay[n] + u for n in range(MODES))
        terms = [states[n] * gain[n] for n in range(MODES)]
        while len(terms) > 1:
            terms = [terms[i] + terms[i + 1] for i in range(0, len(terms), 2)]
        response[pl.ds(t, LANES, stride=PITCH), :] = terms[0]
        return states

    lax.fori_loop(0, ROWS, step, tuple(carried[n] for n in range(MODES)), unroll=4)
    core = place[0]
    for out, parity in ((keep, core), (send, 1 - core)):
        for k in range(HALF // 128):
            j = (k // 2) * 4 + parity * 2 + k % 2
            lanes = pl.ds(pl.multiple_of(j * 128, 128), 128)
            rows = pl.ds(pl.multiple_of(j * PITCH, 8), ROWS)
            out[:, k * 128 : (k + 1) * 128] = (queries[:, lanes] * response[rows, :]).astype(BF16)


def response_call(place, drive, queries, rates, weights, carried):
    whole = pl.BlockSpec(memory_space=pltpu.VMEM)
    return pl.pallas_call(
        response_kernel,
        in_specs=[pl.BlockSpec(memory_space=pltpu.SMEM)] + [whole] * 5,
        out_shape=(jax.ShapeDtypeStruct((ROWS, HALF), BF16), jax.ShapeDtypeStruct((ROWS, HALF), BF16)),
        scratch_shapes=[pltpu.VMEM((LANES * PITCH, 128), F32)],
        compiler_params=pltpu.CompilerParams(vmem_limit_bytes=VMEM_LIMIT),
        cost_estimate=pl.CostEstimate(flops=30_000_000, bytes_accessed=3_000_000, transcendentals=0),
        name="response_and_gate",
    )(place, drive, queries, rates, weights, carried)


def project_kernel(place, *refs):
    weights, gated = refs[: ZL * X], refs[ZL * X : ZL * X + ZH * Y * 2]
    mine, other, left, right, total, w_sem, g_sem = refs[ZL * X + ZH * Y * 2 :]
    z, x, h, y = place[1], place[2], place[3], place[4]
    copies_w, copies_g = [], []
    for i in range(ZH):
        for j in range(Y):
            q = lax.rem(h + i, ZH) * Y + lax.rem(y + Y - j, Y)
            columns = pl.ds(pl.multiple_of(q * HALF, HALF), HALF)
            for part in range(2):
                n = (i * Y + j) * 2 + part
                copy = pltpu.make_async_copy(
                    gated[n], left.at[pl.ds(part * ROWS, ROWS), columns], g_sem.at[n]
                )
                copy.start()
                copies_g.append(copy)
    for s in range(ZL):
        for r in range(X):
            n = s * X + r
            m = lax.rem(z + ZL - s, ZL) * X + lax.rem(x + X - r, X)
            rows = pl.ds(pl.multiple_of(m * ROWS, ROWS), ROWS)
            copy = pltpu.make_async_copy(weights[n], right.at[rows, :], w_sem.at[n])
            copy.start()
            copies_w.append(copy)
    for copy in copies_g:
        copy.wait()
    depth = X * ROWS
    for s in range(ZL):
        for r in range(X):
            copies_w[s * X + r].wait()
        start = pl.multiple_of(lax.rem(z + ZL - s, ZL) * depth, depth)
        for col in range(0, CHANS, 256):
            product = jnp.dot(
                left[:, pl.ds(start, depth)],
                right[pl.ds(start, depth), col : col + 256],
                preferred_element_type=F32,
            )
            if s > 0:
                product += total[:, col : col + 256]
            if s < ZL - 1:
                total[:, col : col + 256] = product
            else:
                mine[:, col : col + 256] = product[:ROWS]
                other[:, col : col + 256] = product[ROWS:].astype(BF16)


def project_call(place, weights, gated):
    count = len(weights) + len(gated)
    whole = pl.BlockSpec(memory_space=pltpu.VMEM)
    return pl.pallas_call(
        project_kernel,
        in_specs=[pl.BlockSpec(memory_space=pltpu.SMEM)] + [pl.BlockSpec(memory_space=pl.ANY)] * count,
        out_specs=(whole, whole),
        out_shape=(jax.ShapeDtypeStruct((ROWS, CHANS), F32), jax.ShapeDtypeStruct((ROWS, CHANS), BF16)),
        scratch_shapes=[
            pltpu.VMEM((2 * ROWS, ZH * Y * HALF), BF16),
            pltpu.VMEM((ZL * X * ROWS, CHANS), BF16),
            pltpu.VMEM((2 * ROWS, CHANS), F32),
            pltpu.SemaphoreType.DMA((len(weights),)),
            pltpu.SemaphoreType.DMA((len(gated),)),
        ],
        compiler_params=pltpu.CompilerParams(vmem_limit_bytes=VMEM_LIMIT),
        cost_estimate=pl.CostEstimate(flops=4_300_000_000, bytes_accessed=14_000_000, transcendentals=0),
        name="projection",
    )(place, *weights, *gated)


def carried_states(ends, rates, z, x, core):
    def decays(steps):
        return jnp.exp(-rates * (ROWS * steps).astype(F32))

    one = jnp.int32(1)
    sibling = swap_core(ends)
    first = jnp.where(core == 0, ends, sibling)
    second = jnp.where(core == 0, sibling, ends)
    chip = decays(one) * first + second
    arrived = [shift_x(chip, r) for r in range(1, X)]
    group = decays(2 * (X - 1 - x)) * chip
    before = jnp.zeros_like(chip)
    for r in range(1, X):
        origin = lax.rem(x + X - r, X)
        group += decays(2 * (X - 1 - origin)) * arrived[r - 1]
        before += jnp.where(r <= x, 1.0, 0.0) * decays(one * 2 * (r - 1)) * arrived[r - 1]
    groups = [ahead_z(group, s) for s in range(1, ZL)]
    far = groups[0]
    for s in range(2, ZL):
        far += decays(one * 2 * X * (s - 1)) * groups[s - 1]
    into_chip = before + decays(2 * x) * far
    return jnp.where(core == 0, into_chip, decays(one) * into_chip + first)


def body(stream, projected, short_taps, decay_rates, residues, out_weight):
    p, q = lax.axis_index("ctx"), lax.axis_index("ch")
    core, x, z = p % CORE, (p // CORE) % X, p // (CORE * X)
    y, h = q % Y, q // Y
    place = jnp.stack([core, z, x, h, y]).astype(jnp.int32)

    proj = projected.transpose(1, 0, 2)
    halo = lax.ppermute(projected[ROWS - 2 :], "ctx", [(i, i + 1) for i in range(ZL * X * CORE - 1)])
    halo = halo.transpose(1, 0, 2).astype(F32)
    drive, queries, ends = drive_call(proj, halo, short_taps.reshape(9, CHANS), decay_rates)

    shards = [out_weight] + [shift_z(out_weight, s) for s in range(1, ZL)]
    weights = []
    for s in range(ZL):
        weights.append(shards[s])
        weights += [shift_x(shards[s], r) for r in range(1, X)]

    rates3 = decay_rates.reshape(MODES, LANES, 128)
    weights3 = residues.reshape(MODES, LANES, 128)
    carried = carried_states(ends, rates3, z, x, core)
    keep, send = response_call(place, drive, queries, rates3, weights3, carried)
    theirs = swap_core(send)

    gated = []
    for part in (keep, theirs):
        across = swap_zh(part)
        gated.append([[v] + [shift_y(v, j) for j in range(1, Y)] for v in (part, across)])
    pieces = [gated[part][i][j] for i in range(ZH) for j in range(Y) for part in range(2)]

    mine, other = project_call(place, weights, pieces)
    summed = stream.astype(F32) + mine + swap_core(other).astype(F32)
    return summed.astype(BF16)


def solution(mesh):
    in_specs = (
        P("ctx", "ch"),
        P("ctx", None, "ch"),
        P(None, None, "ch"),
        P(None, "ch"),
        P(None, "ch"),
        P("ctx", "ch"),
    )
    return jax.shard_map(body, mesh=mesh, in_specs=in_specs, out_specs=P("ctx", "ch"), check_vma=False)
```

```python
import functools

import jax
import jax.numpy as jnp
from jax import lax
from jax.experimental import pallas as pl
from jax.experimental.pallas import tpu as pltpu
from jax.sharding import PartitionSpec as P

F32, BF16 = jnp.float32, jnp.bfloat16
ZL, X, CORE, ZH, Y = 4, 4, 2, 2, 4
ROWS, CHANS, MODES = 256, 1024, 16
LANES = CHANS // 128
PITCH = ROWS + 8
HALF = CHANS // 2
VMEM_LIMIT = 16 * 1024 * 1024


def ctx_pairs(move):
    pairs = []
    for p in range(ZL * X * CORE):
        target = move(p // (X * CORE), (p // CORE) % X, p % CORE)
        if target is not None:
            z, x, c = target
            pairs.append((p, (z * X + x) * CORE + c))
    return pairs


def ch_pairs(move):
    pairs = []
    for q in range(ZH * Y):
        h, y = move(q // Y, q % Y)
        pairs.append((q, h * Y + y))
    return pairs


def swap_core(v):
    return lax.ppermute(v, "ctx", ctx_pairs(lambda z, x, c: (z, x, 1 - c)))


def around_x(v, by):
    return lax.ppermute(v, "ctx", ctx_pairs(lambda z, x, c: (z, (x + by * (1 - 2 * c)) % X, c)))


def around_z(v, by):
    return lax.ppermute(v, "ctx", ctx_pairs(lambda z, x, c: ((z + by * (1 - 2 * c)) % ZL, x, c)))


def flip_x(v, bit):
    return lax.ppermute(v, "ctx", ctx_pairs(lambda z, x, c: (z, x ^ bit, c)))


def flip_z(v, bit):
    return lax.ppermute(v, "ctx", ctx_pairs(lambda z, x, c: (z ^ bit, x, c)))


def ahead_z(v, bit):
    return lax.ppermute(v, "ctx", ctx_pairs(lambda z, x, c: None if z & bit else (z | bit, x, c)))


def swap_zh(v):
    return lax.ppermute(v, "ch", ch_pairs(lambda h, y: (1 - h, y)))


def around_y(v, by):
    pairs = []
    for p in range(ZL * X * CORE):
        step = by * (1 - 2 * (p % CORE))
        for q, target in ch_pairs(lambda h, y: (h, (y + step) % Y)):
            pairs.append((p * ZH * Y + q, p * ZH * Y + target))
    return lax.ppermute(v, ("ctx", "ch"), pairs)


def after(v, *earlier):
    return lax.optimization_barrier((v,) + earlier)[0]


class Lane:
    def __init__(self, *earlier):
        self.earlier = earlier

    def send(self, op, v, *rest):
        result = op(after(v, *self.earlier), *rest)
        self.earlier = (result,)
        return result


def drive_kernel(proj, halo, taps, rates, drive, queries, ends, wide):
    def lane_block(j, carry):
        lanes = pl.ds(pl.multiple_of(j * 128, 128), 128)
        base = pl.multiple_of(j * PITCH, 8)
        for s in range(3):
            wide[s, 6:8, :] = halo[s, :, lanes]
            wide[s, 8:, :] = proj[s, :, lanes].astype(F32)
        step = 64
        for start in range(0, ROWS, step):
            filtered = []
            for s in range(3):
                total = taps[s : s + 1, lanes] * wide[s, 8 + start : 8 + start + step, :]
                total += taps[3 + s : 4 + s, lanes] * wide[s, 7 + start : 7 + start + step, :]
                total += taps[6 + s : 7 + s, lanes] * wide[s, 6 + start : 6 + start + step, :]
                filtered.append(total)
            queries[start : start + step, lanes] = filtered[0]
            drive[pl.ds(base + start, step), :] = filtered[1] * filtered[2]
        lam = [jnp.broadcast_to(rates[n : n + 1, lanes], (8, 128)) for n in range(MODES)]
        decay = [jnp.exp(-8.0 * lam[n]) for n in range(MODES)]

        def rows_block(b, states):
            u = drive[pl.ds(base + b * 8, 8), :]
            return tuple(states[n] * decay[n] + u for n in range(MODES))

        zero = jnp.zeros((8, 128), F32)
        states = lax.fori_loop(0, ROWS // 8, rows_block, (zero,) * MODES, unroll=4)
        left = 7.0 - lax.broadcasted_iota(jnp.int32, (8, 128), 0).astype(F32)
        for n in range(MODES):
            end = jnp.sum(states[n] * jnp.exp(-lam[n] * left), axis=0, keepdims=True)
            ends[n, pl.ds(j, 1), :] = end
        return carry

    lax.fori_loop(0, LANES, lane_block, 0)


def drive_call(proj, halo, taps, rates):
    return pl.pallas_call(
        drive_kernel,
        out_shape=(
            jax.ShapeDtypeStruct((LANES * PITCH, 128), F32),
            jax.ShapeDtypeStruct((ROWS, CHANS), F32),
            jax.ShapeDtypeStruct((MODES, LANES, 128), F32),
        ),
        scratch_shapes=[pltpu.VMEM((3, ROWS + 8, 128), F32)],
        compiler_params=pltpu.CompilerParams(vmem_limit_bytes=VMEM_LIMIT),
        cost_estimate=pl.CostEstimate(flops=1, bytes_accessed=1, transcendentals=0),
        name="drive_and_ends",
    )(proj, halo, taps, rates)


def response_kernel(place, drive, queries, rates, weights, carried, keep, send, response):
    decay = [jnp.exp(-rates[n]) for n in range(MODES)]
    gain = [weights[n] for n in range(MODES)]

    def step(t, states):
        u = drive[pl.ds(t, LANES, stride=PITCH), :]
        states = tuple(states[n] * decay[n] + u for n in range(MODES))
        terms = [states[n] * gain[n] for n in range(MODES)]
        while len(terms) > 1:
            terms = [terms[i] + terms[i + 1] for i in range(0, len(terms), 2)]
        response[pl.ds(t, LANES, stride=PITCH), :] = terms[0]
        return states

    lax.fori_loop(0, ROWS, step, tuple(carried[n] for n in range(MODES)), unroll=4)
    core = place[0]
    for out, parity in ((keep, core), (send, 1 - core)):
        for k in range(HALF // 128):
            j = (k // 2) * 4 + parity * 2 + k % 2
            lanes = pl.ds(pl.multiple_of(j * 128, 128), 128)
            rows = pl.ds(pl.multiple_of(j * PITCH, 8), ROWS)
            out[:, k * 128 : (k + 1) * 128] = (queries[:, lanes] * response[rows, :]).astype(BF16)


def response_call(place, drive, queries, rates, weights, carried):
    whole = pl.BlockSpec(memory_space=pltpu.VMEM)
    return pl.pallas_call(
        response_kernel,
        in_specs=[pl.BlockSpec(memory_space=pltpu.SMEM)] + [whole] * 5,
        out_shape=(jax.ShapeDtypeStruct((ROWS, HALF), BF16), jax.ShapeDtypeStruct((ROWS, HALF), BF16)),
        scratch_shapes=[pltpu.VMEM((LANES * PITCH, 128), F32)],
        compiler_params=pltpu.CompilerParams(vmem_limit_bytes=VMEM_LIMIT),
        cost_estimate=pl.CostEstimate(flops=1, bytes_accessed=1, transcendentals=0),
        name="response_and_gate",
    )(place, drive, queries, rates, weights, carried)


def project_kernel(place, *refs):
    count_w, count_g = ZL * X, Y * 3
    weights, gated = refs[:count_w], refs[count_w : count_w + count_g]
    mine, other, left, total, sem = refs[count_w + count_g :]
    z, x, h, y = place[1], place[2], place[3], place[4]
    sign = 1 - 2 * place[0]

    def origin(at, slot, count):
        return lax.rem(at + count + (0, -1, 1, 2)[slot] * sign, count)

    copies = []

    def put(n, q, first, rows):
        columns = pl.ds(pl.multiple_of(q * HALF, HALF), HALF)
        copy = pltpu.make_async_copy(gated[n], left.at[pl.ds(first, rows), columns], sem.at[n])
        copy.start()
        copies.append(copy)

    for j in range(Y):
        at = origin(y, j, Y)
        put(3 * j, h * Y + at, 0, 2 * ROWS)
        put(3 * j + 1, (1 - h) * Y + at, 0, ROWS)
        put(3 * j + 2, (1 - h) * Y + at, ROWS, ROWS)
    for copy in copies:
        copy.wait()
    for s in range(ZL):
        blocks = [origin(z, s, ZL) * X + origin(x, r, X) for r in range(X)]
        rows = jnp.concatenate([left[:, pl.ds(pl.multiple_of(m * ROWS, ROWS), ROWS)] for m in blocks], axis=1)
        for col in range(0, CHANS, 256):
            shards = [weights[s * X + r][:, col : col + 256] for r in range(X)]
            product = jnp.dot(rows, jnp.concatenate(shards, axis=0), preferred_element_type=F32)
            if s > 0:
                product += total[:, col : col + 256]
            if s < ZL - 1:
                total[:, col : col + 256] = product
            else:
                mine[:, col : col + 256] = product[:ROWS]
                other[:, col : col + 256] = product[ROWS:].astype(BF16)


def project_call(place, weights, gated):
    whole = pl.BlockSpec(memory_space=pltpu.VMEM)
    return pl.pallas_call(
        project_kernel,
        in_specs=[pl.BlockSpec(memory_space=pltpu.SMEM)]
        + [whole] * len(weights)
        + [pl.BlockSpec(memory_space=pl.ANY)] * len(gated),
        out_specs=(whole, whole),
        out_shape=(jax.ShapeDtypeStruct((ROWS, CHANS), F32), jax.ShapeDtypeStruct((ROWS, CHANS), BF16)),
        scratch_shapes=[
            pltpu.VMEM((2 * ROWS, ZH * Y * HALF), BF16),
            pltpu.VMEM((2 * ROWS, CHANS), F32),
            pltpu.SemaphoreType.DMA((Y * 3,)),
        ],
        compiler_params=pltpu.CompilerParams(vmem_limit_bytes=28 * 1024 * 1024),
        cost_estimate=pl.CostEstimate(flops=4_300_000_000, bytes_accessed=14_000_000, transcendentals=0),
        name="projection",
    )(place, *weights, *gated)


def carried_states(ends, rates, z, x, core, before_x, before_z):
    def decays(rows):
        return jnp.exp(-rates * jnp.asarray(rows).astype(F32))

    total, prefix, size, offset = ends, jnp.zeros_like(ends), ROWS, jnp.int32(0)
    steps = (
        (swap_core, core),
        (functools.partial(flip_x, bit=1), x % 2),
        (functools.partial(flip_x, bit=2), x // 2),
        (functools.partial(flip_z, bit=1), z % 2),
        (functools.partial(ahead_z, bit=2), z // 2),
    )
    arrived = []
    for k, (exchange, upper) in enumerate(steps):
        if k == 1:
            total = after(total, *before_x)
        if k == 3:
            total = after(total, *before_z)
        theirs = exchange(total)
        arrived.append(theirs)
        is_upper = upper == 1
        prefix = prefix + jnp.where(is_upper, decays(offset) * theirs, 0.0)
        total = decays(size) * jnp.where(is_upper, theirs, total) + jnp.where(is_upper, total, theirs)
        offset = offset + size * upper
        size = size * 2
    return prefix, arrived[2], arrived[4]


def around(lanes, op, v):
    behind = lanes[0].send(op, v, 1)
    ahead = lanes[1].send(op, v, -1)
    return [v, behind, ahead, lanes[0].send(op, behind, 1)]


def body(stream, projected, short_taps, decay_rates, residues, out_weight):
    p, q = lax.axis_index("ctx"), lax.axis_index("ch")
    core, x, z = p % CORE, (p // CORE) % X, p // (CORE * X)
    y, h = q % Y, q // Y
    place = jnp.stack([core, z, x, h, y]).astype(jnp.int32)

    proj = projected.transpose(1, 0, 2)
    halo = lax.ppermute(projected[ROWS - 2 :], "ctx", [(i, i + 1) for i in range(ZL * X * CORE - 1)])
    z_behind = around_z(out_weight, 1)
    own_behind, own_ahead = around_x(out_weight, 1), around_x(out_weight, -1)
    halo = halo.transpose(1, 0, 2).astype(F32)
    drive, queries, ends = drive_call(proj, halo, short_taps.reshape(9, CHANS), decay_rates)

    rates3 = decay_rates.reshape(MODES, LANES, 128)
    weights3 = residues.reshape(MODES, LANES, 128)
    z_ahead = around_z(after(out_weight, z_behind), -1)
    carried, x_done, z_done = carried_states(ends, rates3, z, x, core, (own_behind, own_ahead), (z_ahead,))
    z_far = around_z(after(z_behind, z_done), 1)

    shards = (out_weight, z_behind, z_ahead, z_far)
    first, second = Lane(x_done), Lane(x_done)
    behind, ahead, far = [own_behind] + [None] * (ZL - 1), [own_ahead] + [None] * (ZL - 1), [None] * ZL
    far[0] = first.send(around_x, behind[0], 1)
    behind[1] = second.send(around_x, shards[1], 1)
    carried = after(carried, far[0], behind[1])
    ahead[1] = first.send(around_x, shards[1], -1)
    far[1] = second.send(around_x, behind[1], 1)
    behind[2] = first.send(around_x, shards[2], 1)
    ahead[2] = second.send(around_x, shards[2], -1)
    far[2] = first.send(around_x, behind[2], 1)
    behind[3] = second.send(around_x, shards[3], 1)
    ahead[3] = first.send(around_x, shards[3], -1)
    far[3] = second.send(around_x, behind[3], 1)
    weights = [v for s in range(ZL) for v in (shards[s], behind[s], ahead[s], far[s])]

    keep, send = response_call(place, drive, queries, rates3, weights3, carried)
    theirs = swap_core(send)
    lane_h, lanes_y = Lane(), (Lane(), Lane())
    across = [lane_h.send(swap_zh, part) for part in (keep, theirs)]
    own = around((Lane(), Lane()), around_y, jnp.concatenate([keep, theirs], axis=0))
    parts = [around(lanes_y if part == 0 else lanes_y[::-1], around_y, across[part]) for part in range(2)]
    pieces = [v for j in range(Y) for v in (own[j], parts[0][j], parts[1][j])]

    mine, other = project_call(place, weights, pieces)
    summed = stream.astype(F32) + mine + swap_core(other).astype(F32)
    return summed.astype(BF16)


def solution(mesh):
    in_specs = (
        P("ctx", "ch"),
        P("ctx", None, "ch"),
        P(None, None, "ch"),
        P(None, "ch"),
        P(None, "ch"),
        P("ctx", "ch"),
    )
    return jax.shard_map(body, mesh=mesh, in_specs=in_specs, out_specs=P("ctx", "ch"), check_vma=False)
```

```python
import functools

import jax
import jax.numpy as jnp
from jax import lax
from jax.experimental import pallas as pl
from jax.experimental.pallas import tpu as pltpu
from jax.sharding import PartitionSpec as P

F32, BF16 = jnp.float32, jnp.bfloat16
ZL, X, CORE, ZH, Y = 4, 4, 2, 2, 4
ROWS, CHANS, MODES = 256, 1024, 16
LANES = CHANS // 128
PITCH = ROWS + 8
HALF = CHANS // 2
VMEM_LIMIT = 16 * 1024 * 1024


def ctx_pairs(move):
    pairs = []
    for p in range(ZL * X * CORE):
        target = move(p // (X * CORE), (p // CORE) % X, p % CORE)
        if target is not None:
            z, x, c = target
            pairs.append((p, (z * X + x) * CORE + c))
    return pairs


def ch_pairs(move):
    pairs = []
    for q in range(ZH * Y):
        h, y = move(q // Y, q % Y)
        pairs.append((q, h * Y + y))
    return pairs


def swap_core(v):
    return lax.ppermute(v, "ctx", ctx_pairs(lambda z, x, c: (z, x, 1 - c)))


def around_x(v, by):
    return lax.ppermute(v, "ctx", ctx_pairs(lambda z, x, c: (z, (x + by * (1 - 2 * c)) % X, c)))


def around_z(v, by):
    return lax.ppermute(v, "ctx", ctx_pairs(lambda z, x, c: ((z + by * (1 - 2 * c)) % ZL, x, c)))


def flip_x(v, bit):
    return lax.ppermute(v, "ctx", ctx_pairs(lambda z, x, c: (z, x ^ bit, c)))


def ahead_z(v, by):
    return lax.ppermute(v, "ctx", ctx_pairs(lambda z, x, c: (z + by, x, c) if z + by < ZL else None))


def swap_zh(v):
    return lax.ppermute(v, "ch", ch_pairs(lambda h, y: (1 - h, y)))


def around_y(v, by):
    pairs = []
    for p in range(ZL * X * CORE):
        step = by * (1 - 2 * (p % CORE))
        for q, target in ch_pairs(lambda h, y: (h, (y + step) % Y)):
            pairs.append((p * ZH * Y + q, p * ZH * Y + target))
    return lax.ppermute(v, ("ctx", "ch"), pairs)


def around(op, v):
    behind, ahead = op(v, 1), op(v, -1)
    return [v, behind, ahead, op(behind, 1)]


def fence(*arrays):
    return lax.optimization_barrier(arrays)


def drive_kernel(proj, halo, taps, rates, drive, queries, ends, wide):
    def lane_block(j, carry):
        lanes = pl.ds(pl.multiple_of(j * 128, 128), 128)
        base = pl.multiple_of(j * PITCH, 8)
        for s in range(3):
            wide[s, 6:8, :] = halo[s, :, lanes]
            wide[s, 8:, :] = proj[s, :, lanes].astype(F32)
        step = 64
        for start in range(0, ROWS, step):
            filtered = []
            for s in range(3):
                total = taps[s : s + 1, lanes] * wide[s, 8 + start : 8 + start + step, :]
                total += taps[3 + s : 4 + s, lanes] * wide[s, 7 + start : 7 + start + step, :]
                total += taps[6 + s : 7 + s, lanes] * wide[s, 6 + start : 6 + start + step, :]
                filtered.append(total)
            queries[start : start + step, lanes] = filtered[0]
            drive[pl.ds(base + start, step), :] = filtered[1] * filtered[2]
        lam = [jnp.broadcast_to(rates[n : n + 1, lanes], (8, 128)) for n in range(MODES)]
        decay = [jnp.exp(-8.0 * lam[n]) for n in range(MODES)]

        def rows_block(b, states):
            u = drive[pl.ds(base + b * 8, 8), :]
            return tuple(states[n] * decay[n] + u for n in range(MODES))

        zero = jnp.zeros((8, 128), F32)
        states = lax.fori_loop(0, ROWS // 8, rows_block, (zero,) * MODES, unroll=4)
        left = 7.0 - lax.broadcasted_iota(jnp.int32, (8, 128), 0).astype(F32)
        for n in range(MODES):
            end = jnp.sum(states[n] * jnp.exp(-lam[n] * left), axis=0, keepdims=True)
            ends[n, pl.ds(j, 1), :] = end
        return carry

    lax.fori_loop(0, LANES, lane_block, 0)


def drive_call(proj, halo, taps, rates):
    return pl.pallas_call(
        drive_kernel,
        out_shape=(
            jax.ShapeDtypeStruct((LANES * PITCH, 128), F32),
            jax.ShapeDtypeStruct((ROWS, CHANS), F32),
            jax.ShapeDtypeStruct((MODES, LANES, 128), F32),
        ),
        scratch_shapes=[pltpu.VMEM((3, ROWS + 8, 128), F32)],
        compiler_params=pltpu.CompilerParams(vmem_limit_bytes=VMEM_LIMIT),
        cost_estimate=pl.CostEstimate(flops=1, bytes_accessed=1, transcendentals=0),
        name="drive_and_ends",
    )(proj, halo, taps, rates)


def response_kernel(place, drive, queries, rates, weights, carried, keep, send, response):
    decay = [jnp.exp(-rates[n]) for n in range(MODES)]
    gain = [weights[n] for n in range(MODES)]

    def step(t, states):
        u = drive[pl.ds(t, LANES, stride=PITCH), :]
        states = tuple(states[n] * decay[n] + u for n in range(MODES))
        terms = [states[n] * gain[n] for n in range(MODES)]
        while len(terms) > 1:
            terms = [terms[i] + terms[i + 1] for i in range(0, len(terms), 2)]
        response[pl.ds(t, LANES, stride=PITCH), :] = terms[0]
        return states

    lax.fori_loop(0, ROWS, step, tuple(carried[n] for n in range(MODES)), unroll=4)
    core = place[0]
    for out, parity in ((keep, core), (send, 1 - core)):
        for k in range(HALF // 128):
            j = (k // 2) * 4 + parity * 2 + k % 2
            lanes = pl.ds(pl.multiple_of(j * 128, 128), 128)
            rows = pl.ds(pl.multiple_of(j * PITCH, 8), ROWS)
            out[:, k * 128 : (k + 1) * 128] = (queries[:, lanes] * response[rows, :]).astype(BF16)


def response_call(place, drive, queries, rates, weights, carried):
    whole = pl.BlockSpec(memory_space=pltpu.VMEM)
    return pl.pallas_call(
        response_kernel,
        in_specs=[pl.BlockSpec(memory_space=pltpu.SMEM)] + [whole] * 5,
        out_shape=(jax.ShapeDtypeStruct((ROWS, HALF), BF16), jax.ShapeDtypeStruct((ROWS, HALF), BF16)),
        scratch_shapes=[pltpu.VMEM((LANES * PITCH, 128), F32)],
        compiler_params=pltpu.CompilerParams(vmem_limit_bytes=VMEM_LIMIT),
        cost_estimate=pl.CostEstimate(flops=1, bytes_accessed=1, transcendentals=0),
        name="response_and_gate",
    )(place, drive, queries, rates, weights, carried)


def project_kernel(place, *refs):
    count_w, count_g = 2 * X, Y * 2
    weights, gated = refs[:count_w], refs[count_w : count_w + count_g]
    mine, other, left, total, sem = refs[count_w + count_g :]

    def shard(s, r, columns):
        first, others = weights[2 * r], weights[2 * r + 1]
        return first[:, columns] if s == 0 else others[(s - 1) * ROWS : s * ROWS, columns]

    z, x, h, y = place[1], place[2], place[3], place[4]
    sign = 1 - 2 * place[0]

    def origin(at, slot, count):
        return lax.rem(at + count + (0, -1, 1, 2)[slot] * sign, count)

    copies = []

    for j in range(Y):
        for i in range(ZH):
            n = 2 * j + i
            q = lax.rem(h + i, ZH) * Y + origin(y, j, Y)
            columns = pl.ds(pl.multiple_of(q * HALF, HALF), HALF)
            copy = pltpu.make_async_copy(gated[n], left.at[:, columns], sem.at[n])
            copy.start()
            copies.append(copy)
    for copy in copies:
        copy.wait()
    for s in range(ZL):
        blocks = [origin(z, s, ZL) * X + origin(x, r, X) for r in range(X)]
        rows = jnp.concatenate([left[:, pl.ds(pl.multiple_of(m * ROWS, ROWS), ROWS)] for m in blocks], axis=1)
        for col in range(0, CHANS, 256):
            shards = [shard(s, r, slice(col, col + 256)) for r in range(X)]
            product = jnp.dot(rows, jnp.concatenate(shards, axis=0), preferred_element_type=F32)
            if s > 0:
                product += total[:, col : col + 256]
            if s < ZL - 1:
                total[:, col : col + 256] = product
            else:
                mine[:, col : col + 256] = product[:ROWS]
                other[:, col : col + 256] = product[ROWS:].astype(BF16)


def project_call(place, weights, gated):
    whole = pl.BlockSpec(memory_space=pltpu.VMEM)
    return pl.pallas_call(
        project_kernel,
        in_specs=[pl.BlockSpec(memory_space=pltpu.SMEM)]
        + [whole] * len(weights)
        + [pl.BlockSpec(memory_space=pl.ANY)] * len(gated),
        out_specs=(whole, whole),
        out_shape=(jax.ShapeDtypeStruct((ROWS, CHANS), F32), jax.ShapeDtypeStruct((ROWS, CHANS), BF16)),
        scratch_shapes=[
            pltpu.VMEM((2 * ROWS, ZH * Y * HALF), BF16),
            pltpu.VMEM((2 * ROWS, CHANS), F32),
            pltpu.SemaphoreType.DMA((Y * 2,)),
        ],
        compiler_params=pltpu.CompilerParams(vmem_limit_bytes=28 * 1024 * 1024),
        cost_estimate=pl.CostEstimate(flops=4_300_000_000, bytes_accessed=14_000_000, transcendentals=0),
        name="projection",
    )(place, *weights, *gated)


def decays(rates, rows):
    return jnp.exp(-rates * jnp.asarray(rows).astype(F32))


def chip_states(ends, rates, core):
    theirs = swap_core(ends)
    first, second = jnp.where(core == 0, ends, theirs), jnp.where(core == 0, theirs, ends)
    return decays(rates, ROWS) * first + second, jnp.where(core == 0, 0.0, theirs)


def ring_states(chip, others, rates, x):
    size = CORE * ROWS
    group, before = decays(rates, size * (X - 1 - x)) * chip, jnp.zeros_like(chip)
    for bits, theirs in zip((1, 2, 3), others):
        at = x ^ bits
        group += decays(rates, size * (X - 1 - at)) * theirs
        before += jnp.where(at < x, decays(rates, size * jnp.maximum(x - 1 - at, 0)) * theirs, 0.0)
    return group, before


def body(stream, projected, short_taps, decay_rates, residues, out_weight):
    p, q = lax.axis_index("ctx"), lax.axis_index("ch")
    core, x, z = p % CORE, (p // CORE) % X, p // (CORE * X)
    y, h = q % Y, q // Y
    place = jnp.stack([core, z, x, h, y]).astype(jnp.int32)

    proj = projected.transpose(1, 0, 2)
    halo = lax.ppermute(projected[ROWS - 2 :], "ctx", [(i, i + 1) for i in range(ZL * X * CORE - 1)])
    z_behind, z_ahead = around_z(out_weight, 1), around_z(out_weight, -1)
    behind0, ahead0 = around_x(out_weight, 1), around_x(out_weight, -1)
    halo = halo.transpose(1, 0, 2).astype(F32)
    drive, queries, ends = drive_call(proj, halo, short_taps.reshape(9, CHANS), decay_rates)

    rates3 = decay_rates.reshape(MODES, LANES, 128)
    weights3 = residues.reshape(MODES, LANES, 128)
    chip, in_chip = chip_states(ends, rates3, core)
    chip, z_behind, behind0, ahead0 = fence(chip, z_behind, behind0, ahead0)
    others = [flip_x(chip, bits) for bits in (1, 2, 3)]
    z_far = around_z(z_behind, 1)
    group, before = ring_states(chip, others, rates3, x)
    group, z_ahead = fence(group, z_ahead)
    groups = [ahead_z(group, by) for by in (1, 2, 3)]
    column = jnp.concatenate([z_behind, z_ahead, z_far], axis=0)
    far1, far2, far3, column, behind0 = fence(*groups, column, behind0)
    behind, ahead = around_x(column, 1), around_x(column, -1)
    groups = [far1, far2, far3]
    later = groups[0]
    for k in (1, 2):
        later += decays(rates3, CORE * X * ROWS * k) * groups[k]
    into_chip = before + decays(rates3, CORE * ROWS * x) * later
    carried = jnp.where(core == 0, into_chip, decays(rates3, ROWS) * into_chip + in_chip)
    keep, send = response_call(place, drive, queries, rates3, weights3, carried)
    both = jnp.concatenate([keep, swap_core(send)], axis=0)
    across = swap_zh(both)
    own = around(around_y, both)
    _, a = fence(own[1], behind)
    far = around_x(a, 1)

    across, _, _ = fence(across, own[1], own[2])
    _, a = fence(ahead, behind0)
    far0 = around_x(a, 1)
    across = around(around_y, across)

    weights = (out_weight, column, behind0, behind, ahead0, ahead, far0, far)
    pieces = [v for j in range(Y) for v in (own[j], across[j])]
    mine, other = project_call(place, weights, pieces)
    summed = stream.astype(F32) + mine + swap_core(other).astype(F32)
    return summed.astype(BF16)


def solution(mesh):
    in_specs = (
        P("ctx", "ch"),
        P("ctx", None, "ch"),
        P(None, None, "ch"),
        P(None, "ch"),
        P(None, "ch"),
        P("ctx", "ch"),
    )
    return jax.shard_map(body, mesh=mesh, in_specs=in_specs, out_specs=P("ctx", "ch"), check_vma=False)
```

```python
import functools

import jax
import jax.numpy as jnp
from jax import lax
from jax.experimental import pallas as pl
from jax.experimental.pallas import tpu as pltpu
from jax.sharding import PartitionSpec as P

F32, BF16 = jnp.float32, jnp.bfloat16
ZL, X, CORE, ZH, Y = 4, 4, 2, 2, 4
ROWS, CHANS, MODES = 256, 1024, 16
LANES = CHANS // 128
PITCH = ROWS + 8
HALF = CHANS // 2
VMEM_LIMIT = 16 * 1024 * 1024


def ctx_pairs(move):
    pairs = []
    for p in range(ZL * X * CORE):
        target = move(p // (X * CORE), (p // CORE) % X, p % CORE)
        if target is not None:
            z, x, c = target
            pairs.append((p, (z * X + x) * CORE + c))
    return pairs


def ch_pairs(move):
    pairs = []
    for q in range(ZH * Y):
        h, y = move(q // Y, q % Y)
        pairs.append((q, h * Y + y))
    return pairs


def swap_core(v):
    return lax.ppermute(v, "ctx", ctx_pairs(lambda z, x, c: (z, x, 1 - c)))


def around_x(v, by):
    return lax.ppermute(v, "ctx", ctx_pairs(lambda z, x, c: (z, (x + by * (1 - 2 * c)) % X, c)))


def around_z(v, by):
    return lax.ppermute(v, "ctx", ctx_pairs(lambda z, x, c: ((z + by * (1 - 2 * c)) % ZL, x, c)))


def flip_x(v, bit):
    return lax.ppermute(v, "ctx", ctx_pairs(lambda z, x, c: (z, x ^ bit, c)))


def ahead_z(v, by):
    return lax.ppermute(v, "ctx", ctx_pairs(lambda z, x, c: (z + by, x, c) if z + by < ZL else None))


def swap_zh(v):
    return lax.ppermute(v, "ch", ch_pairs(lambda h, y: (1 - h, y)))


def around_y(v, by):
    pairs = []
    for p in range(ZL * X * CORE):
        step = by * (1 - 2 * (p % CORE))
        for q, target in ch_pairs(lambda h, y: (h, (y + step) % Y)):
            pairs.append((p * ZH * Y + q, p * ZH * Y + target))
    return lax.ppermute(v, ("ctx", "ch"), pairs)


def around(op, v):
    behind, ahead = op(v, 1), op(v, -1)
    return [v, behind, ahead, op(behind, 1)]


def fence(*arrays):
    return lax.optimization_barrier(arrays)


def drive_kernel(proj, halo, taps, rates, drive, queries, ends, wide):
    def lane_block(j, carry):
        lanes = pl.ds(pl.multiple_of(j * 128, 128), 128)
        base = pl.multiple_of(j * PITCH, 8)
        for s in range(3):
            wide[s, 6:8, :] = halo[s, :, lanes]
            wide[s, 8:, :] = proj[s, :, lanes].astype(F32)
        step = 64
        for start in range(0, ROWS, step):
            filtered = []
            for s in range(3):
                total = taps[s : s + 1, lanes] * wide[s, 8 + start : 8 + start + step, :]
                total += taps[3 + s : 4 + s, lanes] * wide[s, 7 + start : 7 + start + step, :]
                total += taps[6 + s : 7 + s, lanes] * wide[s, 6 + start : 6 + start + step, :]
                filtered.append(total)
            queries[start : start + step, lanes] = filtered[0]
            drive[pl.ds(base + start, step), :] = filtered[1] * filtered[2]
        lam = [jnp.broadcast_to(rates[n : n + 1, lanes], (8, 128)) for n in range(MODES)]
        decay = [jnp.exp(-8.0 * lam[n]) for n in range(MODES)]

        def rows_block(b, states):
            u = drive[pl.ds(base + b * 8, 8), :]
            return tuple(states[n] * decay[n] + u for n in range(MODES))

        zero = jnp.zeros((8, 128), F32)
        states = lax.fori_loop(0, ROWS // 8, rows_block, (zero,) * MODES, unroll=4)
        left = 7.0 - lax.broadcasted_iota(jnp.int32, (8, 128), 0).astype(F32)
        for n in range(MODES):
            end = jnp.sum(states[n] * jnp.exp(-lam[n] * left), axis=0, keepdims=True)
            ends[n, pl.ds(j, 1), :] = end
        return carry

    lax.fori_loop(0, LANES, lane_block, 0)


def drive_call(proj, halo, taps, rates):
    return pl.pallas_call(
        drive_kernel,
        out_shape=(
            jax.ShapeDtypeStruct((LANES * PITCH, 128), F32),
            jax.ShapeDtypeStruct((ROWS, CHANS), F32),
            jax.ShapeDtypeStruct((MODES, LANES, 128), F32),
        ),
        scratch_shapes=[pltpu.VMEM((3, ROWS + 8, 128), F32)],
        compiler_params=pltpu.CompilerParams(vmem_limit_bytes=VMEM_LIMIT),
        cost_estimate=pl.CostEstimate(flops=1, bytes_accessed=1, transcendentals=0),
        name="drive_and_ends",
    )(proj, halo, taps, rates)


def response_kernel(place, drive, queries, rates, weights, carried, keep, send, response):
    decay = [jnp.exp(-rates[n]) for n in range(MODES)]
    gain = [weights[n] for n in range(MODES)]

    def step(t, states):
        u = drive[pl.ds(t, LANES, stride=PITCH), :]
        states = tuple(states[n] * decay[n] + u for n in range(MODES))
        terms = [states[n] * gain[n] for n in range(MODES)]
        while len(terms) > 1:
            terms = [terms[i] + terms[i + 1] for i in range(0, len(terms), 2)]
        response[pl.ds(t, LANES, stride=PITCH), :] = terms[0]
        return states

    lax.fori_loop(0, ROWS, step, tuple(carried[n] for n in range(MODES)), unroll=4)
    core = place[0]
    for out, parity in ((keep, core), (send, 1 - core)):
        for k in range(HALF // 128):
            j = (k // 2) * 4 + parity * 2 + k % 2
            lanes = pl.ds(pl.multiple_of(j * 128, 128), 128)
            rows = pl.ds(pl.multiple_of(j * PITCH, 8), ROWS)
            out[:, k * 128 : (k + 1) * 128] = (queries[:, lanes] * response[rows, :]).astype(BF16)


def response_call(place, drive, queries, rates, weights, carried):
    whole = pl.BlockSpec(memory_space=pltpu.VMEM)
    return pl.pallas_call(
        response_kernel,
        in_specs=[pl.BlockSpec(memory_space=pltpu.SMEM)] + [whole] * 5,
        out_shape=(jax.ShapeDtypeStruct((ROWS, HALF), BF16), jax.ShapeDtypeStruct((ROWS, HALF), BF16)),
        scratch_shapes=[pltpu.VMEM((LANES * PITCH, 128), F32)],
        compiler_params=pltpu.CompilerParams(vmem_limit_bytes=VMEM_LIMIT),
        cost_estimate=pl.CostEstimate(flops=1, bytes_accessed=1, transcendentals=0),
        name="response_and_gate",
    )(place, drive, queries, rates, weights, carried)


def project_kernel(part, place, *refs):
    count_w, count_g = 2 * X, Y * 2
    weights, gated = refs[:count_w], refs[count_w : count_w + count_g]
    out, left, total, sem = refs[count_w + count_g :]

    def shard(s, r, columns):
        first, others = weights[2 * r], weights[2 * r + 1]
        return first[:, columns] if s == 0 else others[(s - 1) * ROWS : s * ROWS, columns]

    z, x, h, y = place[1], place[2], place[3], place[4]
    sign = 1 - 2 * place[0]

    def origin(at, slot, count):
        return lax.rem(at + count + (0, -1, 1, 2)[slot] * sign, count)

    copies = []

    for j in range(Y):
        for i in range(ZH):
            n = 2 * j + i
            q = lax.rem(h + i, ZH) * Y + origin(y, j, Y)
            columns = pl.ds(pl.multiple_of(q * HALF, HALF), HALF)
            copy = pltpu.make_async_copy(gated[n].at[pl.ds(part * ROWS, ROWS), :], left.at[:, columns], sem.at[n])
            copy.start()
            copies.append(copy)
    for copy in copies:
        copy.wait()
    for s in range(ZL):
        blocks = [origin(z, s, ZL) * X + origin(x, r, X) for r in range(X)]
        rows = jnp.concatenate([left[:, pl.ds(pl.multiple_of(m * ROWS, ROWS), ROWS)] for m in blocks], axis=1)
        for col in range(0, CHANS, 256):
            shards = [shard(s, r, slice(col, col + 256)) for r in range(X)]
            product = jnp.dot(rows, jnp.concatenate(shards, axis=0), preferred_element_type=F32)
            if s > 0:
                product += total[:, col : col + 256]
            if s < ZL - 1:
                total[:, col : col + 256] = product
            else:
                out[:, col : col + 256] = product.astype(out.dtype)


def project_call(part, kind, place, weights, gated):
    whole = pl.BlockSpec(memory_space=pltpu.VMEM)
    return pl.pallas_call(
        functools.partial(project_kernel, part),
        in_specs=[pl.BlockSpec(memory_space=pltpu.SMEM)]
        + [whole] * len(weights)
        + [pl.BlockSpec(memory_space=pl.ANY)] * len(gated),
        out_specs=whole,
        out_shape=jax.ShapeDtypeStruct((ROWS, CHANS), kind),
        scratch_shapes=[
            pltpu.VMEM((ROWS, ZH * Y * HALF), BF16),
            pltpu.VMEM((ROWS, CHANS), F32),
            pltpu.SemaphoreType.DMA((Y * 2,)),
        ],
        compiler_params=pltpu.CompilerParams(vmem_limit_bytes=28 * 1024 * 1024),
        cost_estimate=pl.CostEstimate(flops=2_150_000_000, bytes_accessed=10_000_000, transcendentals=0),
        name="projection",
    )(place, *weights, *gated)


def decays(rates, rows):
    return jnp.exp(-rates * jnp.asarray(rows).astype(F32))


def chip_states(ends, rates, core):
    theirs = swap_core(ends)
    first, second = jnp.where(core == 0, ends, theirs), jnp.where(core == 0, theirs, ends)
    return decays(rates, ROWS) * first + second, jnp.where(core == 0, 0.0, theirs)


def ring_states(chip, others, rates, x):
    size = CORE * ROWS
    group, before = decays(rates, size * (X - 1 - x)) * chip, jnp.zeros_like(chip)
    for bits, theirs in zip((1, 2, 3), others):
        at = x ^ bits
        group += decays(rates, size * (X - 1 - at)) * theirs
        before += jnp.where(at < x, decays(rates, size * jnp.maximum(x - 1 - at, 0)) * theirs, 0.0)
    return group, before


def body(stream, projected, short_taps, decay_rates, residues, out_weight):
    p, q = lax.axis_index("ctx"), lax.axis_index("ch")
    core, x, z = p % CORE, (p // CORE) % X, p // (CORE * X)
    y, h = q % Y, q // Y
    place = jnp.stack([core, z, x, h, y]).astype(jnp.int32)

    proj = projected.transpose(1, 0, 2)
    halo = lax.ppermute(projected[ROWS - 2 :], "ctx", [(i, i + 1) for i in range(ZL * X * CORE - 1)])
    z_behind, z_ahead = around_z(out_weight, 1), around_z(out_weight, -1)
    behind0, ahead0 = around_x(out_weight, 1), around_x(out_weight, -1)
    halo = halo.transpose(1, 0, 2).astype(F32)
    drive, queries, ends = drive_call(proj, halo, short_taps.reshape(9, CHANS), decay_rates)

    rates3 = decay_rates.reshape(MODES, LANES, 128)
    weights3 = residues.reshape(MODES, LANES, 128)
    chip, in_chip = chip_states(ends, rates3, core)
    chip, z_behind, behind0, ahead0 = fence(chip, z_behind, behind0, ahead0)
    others = [flip_x(chip, bits) for bits in (1, 2, 3)]
    z_far = around_z(z_behind, 1)
    group, before = ring_states(chip, others, rates3, x)
    group, z_ahead = fence(group, z_ahead)
    groups = [ahead_z(group, by) for by in (1, 2, 3)]
    column = jnp.concatenate([z_behind, z_ahead, z_far], axis=0)
    far1, far2, far3, column, behind0 = fence(*groups, column, behind0)
    behind, ahead = around_x(column, 1), around_x(column, -1)
    groups = [far1, far2, far3]
    later = groups[0]
    for k in (1, 2):
        later += decays(rates3, CORE * X * ROWS * k) * groups[k]
    into_chip = before + decays(rates3, CORE * ROWS * x) * later
    carried = jnp.where(core == 0, into_chip, decays(rates3, ROWS) * into_chip + in_chip)
    keep, send = response_call(place, drive, queries, rates3, weights3, carried)
    both = jnp.concatenate([keep, swap_core(send)], axis=0)
    own = [both, around_y(both, 1), around_y(both, -1)]
    across = swap_zh(both)
    own.append(around_y(own[1], 1))
    _, a = fence(own[1], behind)
    far = around_x(a, 1)

    _, _, across = fence(own[1], own[2], across)
    _, a = fence(ahead, behind0)
    far0 = around_x(a, 1)
    across = around(around_y, across)

    weights = (out_weight, column, behind0, behind, ahead0, ahead, far0, far)
    pieces = [v for j in range(Y) for v in (own[j], across[j])]
    other = swap_core(project_call(1, BF16, place, weights, pieces))
    mine = project_call(0, F32, place, weights, pieces)
    summed = stream.astype(F32) + mine + other.astype(F32)
    return summed.astype(BF16)


def solution(mesh):
    in_specs = (
        P("ctx", "ch"),
        P("ctx", None, "ch"),
        P(None, None, "ch"),
        P(None, "ch"),
        P(None, "ch"),
        P("ctx", "ch"),
    )
    return jax.shard_map(body, mesh=mesh, in_specs=in_specs, out_specs=P("ctx", "ch"), check_vma=False)
```

```python
import functools

import jax
import jax.numpy as jnp
from jax import lax
from jax.experimental import pallas as pl
from jax.experimental.pallas import tpu as pltpu
from jax.sharding import PartitionSpec as P

F32, BF16 = jnp.float32, jnp.bfloat16
ZL, X, CORE, ZH, Y = 4, 4, 2, 2, 4
ROWS, CHANS, MODES = 256, 1024, 16
LANES = CHANS // 128
PITCH = ROWS + 8
HALF = CHANS // 2
VMEM_LIMIT = 16 * 1024 * 1024


def ctx_pairs(move):
    pairs = []
    for p in range(ZL * X * CORE):
        target = move(p // (X * CORE), (p // CORE) % X, p % CORE)
        if target is not None:
            z, x, c = target
            pairs.append((p, (z * X + x) * CORE + c))
    return pairs


def ch_pairs(move):
    pairs = []
    for q in range(ZH * Y):
        h, y = move(q // Y, q % Y)
        pairs.append((q, h * Y + y))
    return pairs


def swap_core(v):
    return lax.ppermute(v, "ctx", ctx_pairs(lambda z, x, c: (z, x, 1 - c)))


def around_x(v, by):
    return lax.ppermute(v, "ctx", ctx_pairs(lambda z, x, c: (z, (x + by * (1 - 2 * c)) % X, c)))


def around_z(v, by):
    return lax.ppermute(v, "ctx", ctx_pairs(lambda z, x, c: ((z + by * (1 - 2 * c)) % ZL, x, c)))


def flip_x(v, bit):
    return lax.ppermute(v, "ctx", ctx_pairs(lambda z, x, c: (z, x ^ bit, c)))


def ahead_z(v, by):
    return lax.ppermute(v, "ctx", ctx_pairs(lambda z, x, c: (z + by, x, c) if z + by < ZL else None))


def swap_zh(v):
    return lax.ppermute(v, "ch", ch_pairs(lambda h, y: (1 - h, y)))


def around_y(v, by):
    pairs = []
    for p in range(ZL * X * CORE):
        step = by * (1 - 2 * (p % CORE))
        for q, target in ch_pairs(lambda h, y: (h, (y + step) % Y)):
            pairs.append((p * ZH * Y + q, p * ZH * Y + target))
    return lax.ppermute(v, ("ctx", "ch"), pairs)


def around(op, v):
    behind, ahead = op(v, 1), op(v, -1)
    return [v, behind, ahead, op(behind, 1)]


def fence(*arrays):
    return lax.optimization_barrier(arrays)


def drive_kernel(proj, halo, taps, rates, drive, queries, ends, wide):
    def lane_block(j, carry):
        lanes = pl.ds(pl.multiple_of(j * 128, 128), 128)
        base = pl.multiple_of(j * PITCH, 8)
        for s in range(3):
            wide[s, 6:8, :] = halo[s, :, lanes]
            wide[s, 8:, :] = proj[s, :, lanes].astype(F32)
        step = 64
        for start in range(0, ROWS, step):
            filtered = []
            for s in range(3):
                total = taps[0, s : s + 1, lanes] * wide[s, 8 + start : 8 + start + step, :]
                total += taps[1, s : s + 1, lanes] * wide[s, 7 + start : 7 + start + step, :]
                total += taps[2, s : s + 1, lanes] * wide[s, 6 + start : 6 + start + step, :]
                filtered.append(total)
            queries[start : start + step, lanes] = filtered[0]
            drive[pl.ds(base + start, step), :] = filtered[1] * filtered[2]
        lam = [jnp.broadcast_to(rates[n : n + 1, lanes], (8, 128)) for n in range(MODES)]
        decay = [jnp.exp(-8.0 * lam[n]) for n in range(MODES)]

        def rows_block(b, states):
            u = drive[pl.ds(base + b * 8, 8), :]
            return tuple(states[n] * decay[n] + u for n in range(MODES))

        zero = jnp.zeros((8, 128), F32)
        states = lax.fori_loop(0, ROWS // 8, rows_block, (zero,) * MODES, unroll=4)
        left = 7.0 - lax.broadcasted_iota(jnp.int32, (8, 128), 0).astype(F32)
        for n in range(MODES):
            end = jnp.sum(states[n] * jnp.exp(-lam[n] * left), axis=0, keepdims=True)
            ends[n, pl.ds(j, 1), :] = end
        return carry

    lax.fori_loop(0, LANES, lane_block, 0)


def drive_call(proj, halo, taps, rates):
    return pl.pallas_call(
        drive_kernel,
        out_shape=(
            jax.ShapeDtypeStruct((LANES * PITCH, 128), F32),
            jax.ShapeDtypeStruct((ROWS, CHANS), F32),
            jax.ShapeDtypeStruct((MODES, LANES, 128), F32),
        ),
        scratch_shapes=[pltpu.VMEM((3, ROWS + 8, 128), F32)],
        compiler_params=pltpu.CompilerParams(vmem_limit_bytes=VMEM_LIMIT),
        cost_estimate=pl.CostEstimate(flops=1, bytes_accessed=1, transcendentals=0),
        name="drive_and_ends",
    )(proj, halo, taps, rates)


def response_kernel(place, drive, queries, rates, weights, carried, keep, send, response):
    decay = [jnp.exp(-rates[n]) for n in range(MODES)]
    gain = [weights[n] for n in range(MODES)]

    def step(t, states):
        u = drive[pl.ds(t, LANES, stride=PITCH), :]
        states = tuple(states[n] * decay[n] + u for n in range(MODES))
        terms = [states[n] * gain[n] for n in range(MODES)]
        while len(terms) > 1:
            terms = [terms[i] + terms[i + 1] for i in range(0, len(terms), 2)]
        response[pl.ds(t, LANES, stride=PITCH), :] = terms[0]
        return states

    lax.fori_loop(0, ROWS, step, tuple(carried[n] for n in range(MODES)), unroll=4)
    core = place[0]
    for out, parity in ((keep, core), (send, 1 - core)):
        for k in range(HALF // 128):
            j = (k // 2) * 4 + parity * 2 + k % 2
            lanes = pl.ds(pl.multiple_of(j * 128, 128), 128)
            rows = pl.ds(pl.multiple_of(j * PITCH, 8), ROWS)
            out[:, k * 128 : (k + 1) * 128] = (queries[:, lanes] * response[rows, :]).astype(BF16)


def response_call(place, drive, queries, rates, weights, carried):
    whole = pl.BlockSpec(memory_space=pltpu.VMEM)
    return pl.pallas_call(
        response_kernel,
        in_specs=[pl.BlockSpec(memory_space=pltpu.SMEM)] + [whole] * 5,
        out_shape=(jax.ShapeDtypeStruct((ROWS, HALF), BF16), jax.ShapeDtypeStruct((ROWS, HALF), BF16)),
        scratch_shapes=[pltpu.VMEM((LANES * PITCH, 128), F32)],
        compiler_params=pltpu.CompilerParams(vmem_limit_bytes=VMEM_LIMIT),
        cost_estimate=pl.CostEstimate(flops=1, bytes_accessed=1, transcendentals=0),
        name="response_and_gate",
    )(place, drive, queries, rates, weights, carried)


def project_kernel(part, place, *refs):
    count_w, count_g = 2 * X, Y * 2
    weights, gated = refs[:count_w], refs[count_w : count_w + count_g]
    out, left, total, sem = refs[count_w + count_g :]

    def shard(s, r, columns):
        first, others = weights[2 * r], weights[2 * r + 1]
        return first[:, columns] if s == 0 else others[(s - 1) * ROWS : s * ROWS, columns]

    z, x, h, y = place[1], place[2], place[3], place[4]
    sign = 1 - 2 * place[0]

    def origin(at, slot, count):
        return lax.rem(at + count + (0, -1, 1, 2)[slot] * sign, count)

    copies = []

    for j in range(Y):
        for i in range(ZH):
            n = 2 * j + i
            q = lax.rem(h + i, ZH) * Y + origin(y, j, Y)
            columns = pl.ds(pl.multiple_of(q * HALF, HALF), HALF)
            copy = pltpu.make_async_copy(gated[n].at[pl.ds(part * ROWS, ROWS), :], left.at[:, columns], sem.at[n])
            copy.start()
            copies.append(copy)
    for copy in copies:
        copy.wait()
    for s in range(ZL):
        blocks = [origin(z, s, ZL) * X + origin(x, r, X) for r in range(X)]
        rows = jnp.concatenate([left[:, pl.ds(pl.multiple_of(m * ROWS, ROWS), ROWS)] for m in blocks], axis=1)
        for col in range(0, CHANS, 256):
            shards = [shard(s, r, slice(col, col + 256)) for r in range(X)]
            product = jnp.dot(rows, jnp.concatenate(shards, axis=0), preferred_element_type=F32)
            if s > 0:
                product += total[:, col : col + 256]
            if s < ZL - 1:
                total[:, col : col + 256] = product
            else:
                out[:, col : col + 256] = product.astype(out.dtype)


def project_call(part, kind, place, weights, gated):
    whole = pl.BlockSpec(memory_space=pltpu.VMEM)
    return pl.pallas_call(
        functools.partial(project_kernel, part),
        in_specs=[pl.BlockSpec(memory_space=pltpu.SMEM)]
        + [whole] * len(weights)
        + [pl.BlockSpec(memory_space=pl.ANY)] * len(gated),
        out_specs=whole,
        out_shape=jax.ShapeDtypeStruct((ROWS, CHANS), kind),
        scratch_shapes=[
            pltpu.VMEM((ROWS, ZH * Y * HALF), BF16),
            pltpu.VMEM((ROWS, CHANS), F32),
            pltpu.SemaphoreType.DMA((Y * 2,)),
        ],
        compiler_params=pltpu.CompilerParams(vmem_limit_bytes=28 * 1024 * 1024),
        cost_estimate=pl.CostEstimate(flops=2_150_000_000, bytes_accessed=10_000_000, transcendentals=0),
        name="projection",
    )(place, *weights, *gated)


def decays(rates, rows):
    return jnp.exp(-rates * jnp.asarray(rows).astype(F32))


def chip_states(ends, rates, core):
    theirs = swap_core(ends)
    first, second = jnp.where(core == 0, ends, theirs), jnp.where(core == 0, theirs, ends)
    return decays(rates, ROWS) * first + second, jnp.where(core == 0, 0.0, theirs)


def ring_states(chip, others, rates, x):
    size = CORE * ROWS
    group, before = decays(rates, size * (X - 1 - x)) * chip, jnp.zeros_like(chip)
    for bits, theirs in zip((1, 2, 3), others):
        at = x ^ bits
        group += decays(rates, size * (X - 1 - at)) * theirs
        before += jnp.where(at < x, decays(rates, size * jnp.maximum(x - 1 - at, 0)) * theirs, 0.0)
    return group, before


def body(stream, projected, short_taps, decay_rates, residues, out_weight):
    p, q = lax.axis_index("ctx"), lax.axis_index("ch")
    core, x, z = p % CORE, (p // CORE) % X, p // (CORE * X)
    y, h = q % Y, q // Y
    place = jnp.stack([core, z, x, h, y]).astype(jnp.int32)

    proj = projected.transpose(1, 0, 2)
    halo = lax.ppermute(projected[ROWS - 2 :], "ctx", [(i, i + 1) for i in range(ZL * X * CORE - 1)])
    z_behind, z_ahead = around_z(out_weight, 1), around_z(out_weight, -1)
    behind0, ahead0 = around_x(out_weight, 1), around_x(out_weight, -1)
    halo = halo.transpose(1, 0, 2).astype(F32)
    drive, queries, ends = drive_call(proj, halo, short_taps, decay_rates)

    rates3 = decay_rates.reshape(MODES, LANES, 128)
    weights3 = residues.reshape(MODES, LANES, 128)
    chip, in_chip = chip_states(ends, rates3, core)
    chip, z_behind, behind0, ahead0 = fence(chip, z_behind, behind0, ahead0)
    others = [flip_x(chip, bits) for bits in (1, 2, 3)]
    z_far = around_z(z_behind, 1)
    group, before = ring_states(chip, others, rates3, x)
    group, z_ahead = fence(group, z_ahead)
    groups = [ahead_z(group, by) for by in (1, 2, 3)]
    column = jnp.concatenate([z_behind, z_ahead, z_far], axis=0)
    far1, far2, far3, column, behind0 = fence(*groups, column, behind0)
    behind, ahead = around_x(column, 1), around_x(column, -1)
    groups = [far1, far2, far3]
    later = groups[0]
    for k in (1, 2):
        later += decays(rates3, CORE * X * ROWS * k) * groups[k]
    into_chip = before + decays(rates3, CORE * ROWS * x) * later
    carried = jnp.where(core == 0, into_chip, decays(rates3, ROWS) * into_chip + in_chip)
    keep, send = response_call(place, drive, queries, rates3, weights3, carried)
    both = jnp.concatenate([keep, swap_core(send)], axis=0)
    own = [both, around_y(both, 1), around_y(both, -1)]
    across = swap_zh(both)
    own.append(around_y(own[1], 1))
    _, a = fence(own[1], behind)
    far = around_x(a, 1)

    _, _, across = fence(own[1], own[2], across)
    _, a = fence(ahead, behind0)
    far0 = around_x(a, 1)
    across = around(around_y, across)

    weights = (out_weight, column, behind0, behind, ahead0, ahead, far0, far)
    pieces = [v for j in range(Y) for v in (own[j], across[j])]
    other = swap_core(project_call(1, BF16, place, weights, pieces))
    mine = project_call(0, F32, place, weights, pieces)
    summed = stream.astype(F32) + mine + other.astype(F32)
    return summed.astype(BF16)


def solution(mesh):
    in_specs = (
        P("ctx", "ch"),
        P("ctx", None, "ch"),
        P(None, None, "ch"),
        P(None, "ch"),
        P(None, "ch"),
        P("ctx", "ch"),
    )
    return jax.shard_map(body, mesh=mesh, in_specs=in_specs, out_specs=P("ctx", "ch"), check_vma=False)
```
